32 devices in a mesh: dp: 4 (over x, core), expert: 8 (over z, y).
Axes of the slice: x: 2, y: 2, z: 4, core: 2. Of those that a mesh axis runs over, the one named last changes fastest.
Arguments:
- tokens: bfloat16 [4096, 768], P(('dp', 'expert')), may hold values from -6 to 6
- cotangent: bfloat16 [4096, 768], P(('dp', 'expert')), may hold values from -6 to 6
- doc_ids: int32 [64, 64], P(('dp', 'expert')), may hold values from 0 to 2, never falling along the last dimension, each value on 1 to 48 neighbouring positions
- expert_ids: int32 [4096, 2], P(('dp', 'expert')), may hold values from 0 to 31, all different within a row; in each aligned block of 64 rows (0 to 63, 64 to 127, ...) at most 5 rows name the same one
- gate_logits: float32 [4096, 2], P(('dp', 'expert')), may hold values from -6 to 6
- gain_attn_a: bfloat16 [768], P(('dp', 'expert')), may hold values from 0.5 to 1.5
- gain_mlp: bfloat16 [768], P(('dp', 'expert')), may hold values from 0.5 to 1.5
- gain_attn_b: bfloat16 [768], P(('dp', 'expert')), may hold values from 0.5 to 1.5
- gain_moe: bfloat16 [768], P(('dp', 'expert')), may hold values from 0.5 to 1.5
- bias_a: bfloat16 [384], P(('dp', 'expert')), may hold values from -4 to 4
- bias_b: bfloat16 [384], P(('dp', 'expert')), may hold values from -4 to 4
- qkv_a: bfloat16 [768, 2304], P(('dp', 'expert')), may hold values from -0.21875 to 0.21875
- out_a: bfloat16 [768, 768], P(('dp', 'expert')), may hold values from -0.875 to 0.875
- w_gate: bfloat16 [768, 3072], P(('dp', 'expert')), may hold values from -0.21875 to 0.21875
- w_up: bfloat16 [768, 3072], P(('dp', 'expert')), may hold values from -0.21875 to 0.21875
- w_down: bfloat16 [3072, 768], P(('dp', 'expert')), may hold values from -0.15625 to 0.15625
- qkv_b: bfloat16 [768, 2304], P(('dp', 'expert')), may hold values from -0.21875 to 0.21875
- out_b: bfloat16 [768, 768], P(('dp', 'expert')), may hold values from -0.875 to 0.875
- expert_in: bfloat16 [32, 768, 3072], P('expert', None, 'dp'), may hold values from -0.21875 to 0.21875
- expert_out: bfloat16 [32, 3072, 768], P('expert', 'dp'), may hold values from -0.15625 to 0.15625
Outputs:
- out: bfloat16 [4096, 768], P(('dp', 'expert'))
- grad_tokens: float32 [4096, 768], P(('dp', 'expert'))
- grad_gain_attn_a: float32 [768], P(('dp', 'expert'))
- grad_gain_mlp: float32 [768], P(('dp', 'expert'))
- grad_gain_attn_b: float32 [768], P(('dp', 'expert'))
- grad_gain_moe: float32 [768], P(('dp', 'expert'))
- grad_bias_a: float32 [384], P(('dp', 'expert'))
- grad_bias_b: float32 [384], P(('dp', 'expert'))
- grad_qkv_a: float32 [768, 2304], P(('dp', 'expert'))
- grad_out_a: float32 [768, 768], P(('dp', 'expert'))
- grad_w_gate: float32 [768, 3072], P(('dp', 'expert'))
- grad_w_up: float32 [768, 3072], P(('dp', 'expert'))
- grad_w_down: float32 [3072, 768], P(('dp', 'expert'))
- grad_qkv_b: float32 [768, 2304], P(('dp', 'expert'))
- grad_out_b: float32 [768, 768], P(('dp', 'expert'))
- grad_expert_in: float32 [32, 768, 3072], P('expert', None, 'dp')
- grad_expert_out: float32 [32, 3072, 768], P('expert', 'dp')
The draws below stay inside these ranges and needn't reach their ends.
Inputs may be any that keep to these rules, and one draw needn't show every extreme that they name: `expert_ids`: each row names two different experts; in each aligned block of 64 rows (one micro-batch of one device) no expert is named by more than 5 rows, a bound that some block reaches. `doc_ids`: within each row, document numbers never fall; a document holds 1 to 64 - 64 // 4 positions, and one holds exactly that many.
All inputs are finite; a program needn't handle non-finite values.
Results may differ from the reference program's by a relative error of at most 0.02.
Values may be sent and summed in bfloat16 or wider, within the bound.
A program may use at most 256 MiB of HBM per device.

```python
import math
import jax
import jax.numpy as jnp
import numpy as np
from jax import lax

D = 768
HEADS = 12
HEAD_DIM = 64
FF = 3072
BUCKETS = 32
ROWS = 64
EXPERTS = 32
CAP = 5
BLOCKS = 64
TOKENS = 4096


def block_scale(key, dims, split, least, top_value):
    loudness = 1.0
    for position, blocks in split:
        steps = jax.random.uniform(jax.random.fold_in(jax.random.fold_in(key, 6), position), (blocks,), jnp.float32, least / len(split), top_value / len(split))
        loudness = loudness * jnp.repeat(jnp.exp(steps), dims[position] // blocks).reshape((-1,) + (1,) * (len(dims) - 1 - position))
    return loudness


def split_up(number_of, total, most, skew):
    portions = [(1 << 20) // math.isqrt(rank ** skew) + 1 for rank in range(2, number_of + 1)]
    rest, holding = total - most - (number_of - 1), [1] * (number_of - 1)
    while rest > 0:
        movable = [i for i in range(number_of - 1) if holding[i] < most]
        mass, remaining = sum([portions[i] for i in movable]), rest
        for i in movable:
            more = min(most - holding[i], max(1, remaining * portions[i] // mass), rest)
            holding[i] = holding[i] + more
            rest = rest - more
    return np.array([most] + holding)


def ragged(own_key, count, total, most, slope):
    if count == 2:
        one = jax.random.randint(own_key, (), max(1, total - most), min(most, total - 1) + 1)
        return jnp.stack([one, total - one])
    tallies = jnp.asarray(split_up(count, total, most, slope), jnp.int32)
    couples = (count - 1) // 2
    source_of, sink = tallies[1:1 + 2 * couples:2], tallies[2:2 + 2 * couples:2]
    margin = jnp.minimum(source_of - 1, most - sink)
    passed = jax.random.randint(jax.random.fold_in(own_key, 1), (couples,), 0, 1 << 20) % (margin + 1)
    tallies = tallies.at[1:1 + 2 * couples:2].set(source_of - passed).at[2:2 + 2 * couples:2].set(sink + passed)
    return tallies[jax.random.permutation(jax.random.fold_in(own_key, 2), count)]


def routed_block(own_key, own, number, rows, amount, top, most, slope):
    sequence = jax.random.permutation(own_key, amount)
    crowded, common = portions_of(amount, rows * top, most, slope, True), portions_of(amount, rows * top, most, slope, False)
    places = jnp.arange(amount)

    def named(sizes, offset_by):
        used = int((sizes > 0).sum())
        fixed = max(1, used // 4)
        shifted = fixed + (places - fixed + offset_by * (used - fixed)) % max(1, amount - fixed)
        return jnp.zeros((amount,), jnp.int32).at[sequence[jnp.where(places < fixed, places, shifted)]].set(jnp.asarray(sizes, jnp.int32))

    sizes = jnp.where(number % 4 == 0, named(crowded, number // 4), named(common, number - number // 4 - 1))
    mixed = jax.random.permutation(jax.random.fold_in(own, 3), amount)
    donor, sink = mixed[0:amount // 2 * 2:2], mixed[1:amount // 2 * 2:2]
    slack = jnp.minimum(sizes[donor] - 1, most - sizes[sink]) // 2
    slack = jnp.where((donor == sequence[0]) | (sink == sequence[0]) | (sizes[sink] == 0), 0, jnp.maximum(slack, 0))
    shifted = jax.random.randint(jax.random.fold_in(own, 4), (amount // 2,), 0, 1 << 20) % (slack + 1)
    sizes = sizes.at[donor].add(-shifted).at[sink].add(shifted)
    labels = jnp.searchsorted(jnp.cumsum(sizes), jnp.arange(rows * top), side="right").astype(jnp.int32)
    table = labels.reshape(top, rows).T
    table = table[jax.random.permutation(jax.random.fold_in(own, 1), rows)]
    offset_by = jax.random.randint(jax.random.fold_in(own, 2), (rows, 1), 0, top)
    return jnp.take_along_axis(table, (jnp.arange(top)[None, :] + offset_by) % top, axis=1)


def portions_of(amount, total, bound, slope, full):
    weights = [(1 << 20) // math.isqrt(rank ** slope) + 1 for rank in range(1, amount + 1)]
    largest = bound if full else min(bound, max(-(-total // amount), total * weights[0] // sum(weights)))
    least = 1 if total - largest >= amount - 1 else 0
    given, rest = [largest] + [least] * (amount - 1), total - largest - least * (amount - 1)
    while rest > 0:
        free = [i for i in range(1, amount) if given[i] < largest] or [i for i in range(1, amount) if given[i] < bound]
        pool, budget = sum([weights[i] for i in free]), rest
        for i in free:
            addition = min(bound - given[i], max(1, budget * weights[i] // pool), rest)
            given[i] = given[i] + addition
            rest = rest - addition
    return np.array(given)


def bell_draw(own_key, dims, deviation, limit, split=(), kind=jnp.bfloat16):
    drawn = jax.random.normal(own_key, dims, jnp.float32) * deviation
    if len(split) > 0:
        drawn = block_scale(own_key, dims, split, -0.22, 0.18) * drawn
    return jnp.clip(drawn, min=-limit, max=limit).astype(kind)


def setup_inputs(seed: int = 0) -> dict:
    key_of = jax.random.split(jax.random.key(seed), 21)
    tokens = bell_draw(key_of[0], (TOKENS, D), 1.0, 6.0, ((0, 32),))
    cotangent = bell_draw(key_of[1], (TOKENS, D), 1.0, 6.0, ((0, 32),))
    doc_ids = jax.vmap(lambda own: jnp.searchsorted(jnp.cumsum(ragged(own, 3, ROWS, ROWS - ROWS // 4, 1)), jnp.arange(ROWS), side="right"))(jax.random.split(key_of[2], BLOCKS)).reshape((BLOCKS, ROWS)).astype(jnp.int32)
    expert_ids_keys = jax.random.split(jax.random.fold_in(key_of[3], 1), TOKENS // ROWS)
    expert_ids_turns = jax.random.permutation(jax.random.fold_in(key_of[3], 3), TOKENS // ROWS)
    expert_ids = jax.vmap(lambda own, number: routed_block(jax.random.fold_in(key_of[3], 2), own, number, ROWS, EXPERTS, 2, CAP, 2))(expert_ids_keys, expert_ids_turns).reshape((TOKENS, 2))
    gate_logits = bell_draw(key_of[4], (TOKENS, 2), 1.0, 6.0, ((0, 32),), jnp.float32)
    gain_attn_a = jnp.clip(1.0 + 0.1 * jax.random.normal(key_of[5], (D,), jnp.float32), 0.5, 1.5).astype(jnp.bfloat16)
    gain_mlp = jnp.clip(1.0 + 0.1 * jax.random.normal(key_of[6], (D,), jnp.float32), 0.5, 1.5).astype(jnp.bfloat16)
    gain_attn_b = jnp.clip(1.0 + 0.1 * jax.random.normal(key_of[7], (D,), jnp.float32), 0.5, 1.5).astype(jnp.bfloat16)
    gain_moe = jnp.clip(1.0 + 0.1 * jax.random.normal(key_of[8], (D,), jnp.float32), 0.5, 1.5).astype(jnp.bfloat16)
    bias_a = bell_draw(key_of[9], (HEADS * BUCKETS,), 1.0, 4.0, ((0, 32),))
    bias_b = bell_draw(key_of[10], (HEADS * BUCKETS,), 1.0, 4.0, ((0, 32),))
    qkv_a = bell_draw(key_of[11], (D, 3 * D), D ** -0.5, 0.21875, ((0, 32),))
    out_a = bell_draw(key_of[12], (D, D), (D // 16) ** -0.5, 0.875, ((0, 32),))
    w_gate = bell_draw(key_of[13], (D, FF), D ** -0.5, 0.21875, ((0, 32),))
    w_up = bell_draw(key_of[14], (D, FF), D ** -0.5, 0.21875, ((0, 32),))
    w_down = bell_draw(key_of[15], (FF, D), (FF // 2) ** -0.5, 0.15625, ((0, 32),))
    qkv_b = bell_draw(key_of[16], (D, 3 * D), D ** -0.5, 0.21875, ((0, 32),))
    out_b = bell_draw(key_of[17], (D, D), (D // 16) ** -0.5, 0.875, ((0, 32),))
    expert_in = bell_draw(key_of[18], (EXPERTS, D, FF), D ** -0.5, 0.21875, ((0, 8), (2, 4)))
    expert_out = bell_draw(key_of[19], (EXPERTS, FF, D), (FF // 2) ** -0.5, 0.15625, ((0, 8), (1, 4)))
    return {"tokens": tokens, "cotangent": cotangent, "doc_ids": doc_ids, "expert_ids": expert_ids, "gate_logits": gate_logits, "gain_attn_a": gain_attn_a, "gain_mlp": gain_mlp, "gain_attn_b": gain_attn_b, "gain_moe": gain_moe, "bias_a": bias_a, "bias_b": bias_b, "qkv_a": qkv_a, "out_a": out_a, "w_gate": w_gate, "w_up": w_up, "w_down": w_down, "qkv_b": qkv_b, "out_b": out_b, "expert_in": expert_in, "expert_out": expert_out}


@jax.custom_vjp
def low(v):
    return lax.optimization_barrier(v.astype(jnp.bfloat16)).astype(jnp.float32)

@jax.custom_vjp
def low_back(v):
    return v

def low_keep(v):
    return (low(v), None)

def low_pass(kept, grad):
    return (grad,)

def back_keep(v):
    return (v, None)

def back_low(kept, grad):
    return (low(grad),)
low.defvjp(low_keep, low_pass)
low_back.defvjp(back_keep, back_low)
HIGH = lax.Precision.HIGHEST

def rms(values):
    return values * lax.rsqrt(lax.optimization_barrier(jnp.mean(values * values, axis=-1, keepdims=True)) + 1e-06)

def layout(docs):
    place = jnp.arange(ROWS, dtype=jnp.int32)
    apart = place[:, None] - place[None, :]
    allowed = (apart >= 0) & (docs[:, None] == docs[None, :])
    bucket = jnp.clip(apart, 0, BUCKETS - 1).astype(jnp.int32)
    return (allowed, bucket)

def attention(rows, docs, gain, bias, wqkv, wout):
    allowed, bucket = layout(docs)
    normed = low(rms(rows) * gain)
    mixed = low_back(low(jnp.dot(normed, wqkv, precision=HIGH)))
    queries = mixed[:, :D].reshape(ROWS, HEADS, HEAD_DIM)
    keys = mixed[:, D:2 * D].reshape(ROWS, HEADS, HEAD_DIM)
    values = mixed[:, 2 * D:].reshape(ROWS, HEADS, HEAD_DIM)
    scores = jnp.einsum('qhd,khd->hqk', queries, keys, precision=HIGH) * (1.0 / math.sqrt(HEAD_DIM))
    scores = scores + bias.reshape(HEADS, BUCKETS)[:, bucket]
    scores = low_back(jnp.where(allowed[None], scores, -1000000000.0))
    attend = jax.nn.softmax(scores, axis=-1)
    context = jnp.einsum('hqk,khd->qhd', low(attend), values, precision=HIGH).reshape(ROWS, D)
    context = low_back(low(context))
    return low_back(jnp.dot(context, wout, precision=HIGH))

def feed(rows, gain, w_gate, w_up, w_down):
    normed = low(rms(rows) * gain)
    gate = low_back(jnp.dot(normed, w_gate, precision=HIGH))
    up = low_back(jnp.dot(normed, w_up, precision=HIGH))
    hidden = low(jax.nn.gelu(gate, approximate=False) * up)
    return low_back(jnp.dot(hidden, w_down, precision=HIGH))

def slot_of(ids):
    flat = ids.reshape(-1)
    hits = (flat[:, None] == jnp.arange(EXPERTS, dtype=jnp.int32)[None, :]).astype(jnp.int32)
    before = jnp.cumsum(hits, axis=0) - hits
    return lax.optimization_barrier(jnp.sum(before * hits, axis=1)).reshape(ROWS, 2).astype(jnp.int32)

def reference(tokens, cotangent, doc_ids, expert_ids, gate_logits, gain_attn_a, gain_mlp, gain_attn_b, gain_moe, bias_a, bias_b, qkv_a, out_a, w_gate, w_up, w_down, qkv_b, out_b, expert_in, expert_out):
    params = tuple((item.astype(jnp.float32) for item in (gain_attn_a, gain_mlp, gain_attn_b, gain_moe, bias_a, bias_b, qkv_a, out_a, w_gate, w_up, w_down, qkv_b, out_b, expert_in, expert_out)))
    start = tokens.astype(jnp.float32).reshape(BLOCKS, ROWS, D)
    ids = expert_ids.reshape(BLOCKS, ROWS, 2).astype(jnp.int32)
    mix = jax.nn.softmax(gate_logits.astype(jnp.float32).reshape(BLOCKS, ROWS, 2), axis=-1)
    slots = jax.vmap(slot_of)(ids)
    block_index = jnp.broadcast_to(jnp.arange(BLOCKS, dtype=jnp.int32)[:, None, None], (BLOCKS, ROWS, 2))

    def forward(inputs, weights):
        g_a, g_m, g_b, g_e, b_a, b_b, wq_a, wo_a, wg, wu, wd, wq_b, wo_b, w_in, w_out = weights

        def dense_layer(item):
            rows, docs = item
            first = rows + attention(rows, docs, g_a, b_a, wq_a, wo_a)
            return first + feed(first, g_m, wg, wu, wd)

        def second_attention(item):
            rows, docs = item
            return rows + attention(rows, docs, g_b, b_b, wq_b, wo_b)
        middle = lax.map(jax.checkpoint(dense_layer), (inputs, doc_ids))
        mixed_rows = lax.map(jax.checkpoint(second_attention), (middle, doc_ids))
        normed = low(rms(mixed_rows) * g_e)
        spread = jnp.broadcast_to(normed[:, :, None, :], (BLOCKS, ROWS, 2, D))
        buffer = jnp.zeros((BLOCKS, CAP, EXPERTS, D), jnp.float32).at[block_index, slots, ids].add(spread)
        buffer = low_back(buffer)
        flat = buffer.transpose(2, 0, 1, 3).reshape(EXPERTS, BLOCKS * CAP, D)

        def one_expert(item):
            rows, first_w, second_w = item
            pre = low_back(jnp.dot(rows, first_w, precision=HIGH))
            act = low(jax.nn.gelu(pre, approximate=False))
            return jnp.dot(act, second_w, precision=HIGH)
        answered = lax.map(jax.checkpoint(one_expert), (flat, w_in, w_out))
        answered = low_back(low(answered))
        slots_back = answered.reshape(EXPERTS, BLOCKS, CAP, D).transpose(1, 2, 0, 3)
        routed = slots_back[block_index, slots, ids]
        return mixed_rows + lax.optimization_barrier(jnp.sum(routed * mix[..., None], axis=2))
    result, pull = jax.vjp(forward, start, params)
    grad_start, grads = pull(cotangent.astype(jnp.float32).reshape(BLOCKS, ROWS, D))
    return (result.reshape(TOKENS, D).astype(jnp.bfloat16), grad_start.reshape(TOKENS, D), grads[0], grads[1], grads[2], grads[3], grads[4], grads[5], grads[6], grads[7], grads[8], grads[9], grads[10], grads[11], grads[12], grads[13], grads[14])
```

```python
import functools
import math

import jax
import jax.numpy as jnp
from jax import lax
from jax.experimental import pallas as pl
from jax.experimental.pallas import tpu as pltpu
from jax.sharding import PartitionSpec as P

D = 768
HEADS = 12
HEAD_DIM = 64
BUCKETS = 32
EXP_DEV = 4
ROWS = 64
MICRO = 2
AXES = ("dp", "expert")
MESH = pl.DeviceIdType.MESH

EPSILON = 1e-06
ROOT_HALF = 0.7071067811865476
ROOT_TWO_PI = 0.3989422804014327
FACTOR = 1.0 / math.sqrt(HEAD_DIM)


class Cube:
    def __init__(self, dp, expert):
        self.low = expert.bit_length() - 1
        self.bits = (dp * expert).bit_length() - 1
        self.sizes = (dp, expert)
        self.core = self.bits - self.low - 1

    def coordinates(self):
        dp, expert = lax.axis_index("dp"), lax.axis_index("expert")
        out = []
        for bit in range(self.bits):
            shift = self.bits - 1 - bit
            if shift >= self.low:
                out.append(lax.rem(lax.div(dp, 1 << (shift - self.low)), 2))
            else:
                out.append(lax.rem(lax.div(expert, 1 << shift), 2))
        return out

    def partner(self, bit, here):
        dp, expert = lax.axis_index("dp"), lax.axis_index("expert")
        shift = self.bits - 1 - bit
        if shift >= self.low:
            step = 1 << (shift - self.low)
            return (dp + step - 2 * step * here[bit], expert)
        step = 1 << shift
        return (dp, expert + step - 2 * step * here[bit])

    def orders(self):
        others = [bit for bit in range(self.core)]
        inner = [bit for bit in range(self.core + 1, self.bits)]
        first = inner[:-1] + inner[-1:] + others + [self.core]
        second = inner[:-1] + others + inner[-1:] + [self.core]
        return (first, second)

    def greet(self, here):
        barrier = pltpu.get_barrier_semaphore()
        for bit in range(self.bits):
            pl.semaphore_signal(
                barrier, inc=1, device_id=self.partner(bit, here), device_id_type=MESH
            )
        pl.semaphore_wait(barrier, self.bits)


def gather_kernel(cube, count, *refs):
    sources, outs = refs[:count], refs[count : 2 * count]
    local_sem, send_sem, recv_sem = refs[2 * count :]
    here = cube.coordinates()
    orders = cube.orders()
    own = []
    for index in range(count):
        copy = pltpu.make_async_copy(
            sources[index], outs[index].at[tuple(here)], local_sem.at[index]
        )
        copy.start()
        own.append(copy)
    cube.greet(here)
    going = [None] * count
    for tick in range(cube.bits + (count - 1) // 2 + 1):
        for index in range(count):
            stage = tick - index // 2
            if not 0 <= stage <= cube.bits:
                continue
            if stage == 0:
                own[index].wait()
            else:
                going[index].wait()
            if stage == cube.bits:
                continue
            order = orders[index % 2]
            done = order[:stage]
            place = tuple(slice(None) if b in done else here[b] for b in range(cube.bits))
            block = outs[index].at[place]
            copy = pltpu.make_async_remote_copy(
                src_ref=block,
                dst_ref=block,
                send_sem=send_sem.at[index, stage],
                recv_sem=recv_sem.at[index, stage],
                device_id=cube.partner(order[stage], here),
                device_id_type=MESH,
            )
            copy.start()
            going[index] = copy


def gather_all(cube, shards):
    count = len(shards)
    lead = (2,) * cube.bits
    full = pl.pallas_call(
        functools.partial(gather_kernel, cube, count),
        out_shape=[jax.ShapeDtypeStruct(lead + s.shape, s.dtype) for s in shards],
        in_specs=[pl.BlockSpec(memory_space=pl.ANY)] * count,
        out_specs=[pl.BlockSpec(memory_space=pl.ANY)] * count,
        scratch_shapes=[
            pltpu.SemaphoreType.DMA((count,)),
            pltpu.SemaphoreType.DMA((count, cube.bits)),
            pltpu.SemaphoreType.DMA((count, cube.bits)),
        ],
        compiler_params=pltpu.CompilerParams(collective_id=0, has_side_effects=True),
    )(*shards)
    return [f.reshape((-1,) + f.shape[-1:]) for f in full]


def reduce_kernel(cube, count, *refs):
    sources, outs = refs[:count], refs[count : 2 * count]
    rest = refs[2 * count :]
    totals = rest[:count]
    slots = [
        rest[count + index * cube.bits : count + (index + 1) * cube.bits] for index in range(count)
    ]
    local_sem, send_sem, recv_sem = rest[count + count * cube.bits :]
    here = cube.coordinates()
    orders = [list(reversed(order)) for order in cube.orders()]
    core = cube.core
    own = []
    for index in range(count):
        place = tuple(here[b] if b == core else slice(None) for b in range(cube.bits))
        copy = pltpu.make_async_copy(
            sources[index].at[place], totals[index], local_sem.at[index]
        )
        copy.start()
        own.append(copy)
    cube.greet(here)
    going = [None] * count
    others = [b for b in range(cube.bits) if b != core]

    def add(index, stage):
        order = orders[index % 2]
        done = order[: stage + 1]
        live = [b for b in others if b not in done]
        slot, total = slots[index][stage], totals[index]
        if not live:
            outs[index][...] = total[tuple(here[b] for b in others)].astype(jnp.float32) + slot[
                ...
            ].astype(jnp.float32)
            return

        def step(k, carry):
            where, inner = {}, []
            for position, b in enumerate(live):
                where[b] = lax.rem(lax.div(k, 1 << (len(live) - 1 - position)), 2)
                inner.append(where[b])
            at = tuple(where[b] if b in where else here[b] for b in others)
            left = total[at].astype(jnp.float32)
            right = slot[tuple(inner)].astype(jnp.float32)
            total[at] = (left + right).astype(total.dtype)
            return carry

        lax.fori_loop(0, 1 << len(live), step, 0)

    for tick in range(cube.bits + (count - 1) // 2 + 1):
        for index in range(count):
            stage = tick - index // 2
            if not 0 <= stage <= cube.bits:
                continue
            order = orders[index % 2]
            if stage > 0:
                if stage == 1:
                    own[index].wait()
                going[index].wait()
                add(index, stage - 1)
            if stage == cube.bits:
                continue
            bit = order[stage]
            done = order[:stage]
            if stage == 0:
                place = tuple(1 - here[b] if b == bit else slice(None) for b in range(cube.bits))
                block = sources[index].at[place]
            else:
                place = tuple(
                    1 - here[b] if b == bit else (here[b] if b in done else slice(None))
                    for b in others
                )
                block = totals[index].at[place]
            copy = pltpu.make_async_remote_copy(
                src_ref=block,
                dst_ref=slots[index][stage],
                send_sem=send_sem.at[index, stage],
                recv_sem=recv_sem.at[index, stage],
                device_id=cube.partner(bit, here),
                device_id_type=MESH,
            )
            copy.start()
            going[index] = copy


def reduce_all(cube, wholes):
    count = len(wholes)
    lead = (2,) * cube.bits
    shapes = [w.shape[1:] for w in wholes]
    wholes = [w.reshape(lead + w.shape[1:]) for w in wholes]
    scratch = [
        pltpu.VMEM((2,) * (cube.bits - 1) + shape, w.dtype) for shape, w in zip(shapes, wholes)
    ]
    for shape, w in zip(shapes, wholes):
        for stage in range(cube.bits):
            scratch.append(pltpu.VMEM((2,) * (cube.bits - 1 - stage) + shape, w.dtype))
    return pl.pallas_call(
        functools.partial(reduce_kernel, cube, count),
        out_shape=[jax.ShapeDtypeStruct(shape, jnp.float32) for shape in shapes],
        in_specs=[pl.BlockSpec(memory_space=pl.ANY)] * count,
        out_specs=[pl.BlockSpec(memory_space=pltpu.VMEM)] * count,
        scratch_shapes=scratch
        + [
            pltpu.SemaphoreType.DMA((count,)),
            pltpu.SemaphoreType.DMA((count, cube.bits)),
            pltpu.SemaphoreType.DMA((count, cube.bits)),
        ],
        compiler_params=pltpu.CompilerParams(
            collective_id=1, has_side_effects=True, vmem_limit_bytes=58 * 2**20
        ),
    )(*wholes)


def product(left, right):
    return jnp.dot(left, right, preferred_element_type=jnp.float32)


def product_left(left, right):
    return lax.dot_general(
        left, right, (((0,), (0,)), ((), ())), preferred_element_type=jnp.float32
    )


def product_right(left, right):
    return lax.dot_general(
        left, right, (((1,), (1,)), ((), ())), preferred_element_type=jnp.float32
    )


def einsum(spec, left, right):
    return jnp.einsum(spec, left, right, preferred_element_type=jnp.float32)


def gelu_slope(values):
    return (
        0.5 * (1.0 + lax.erf(values * ROOT_HALF))
        + values * jnp.exp(-0.5 * values * values) * ROOT_TWO_PI
    )


def normalize(rows, gain):
    scale = lax.rsqrt(jnp.mean(rows * rows, axis=-1, keepdims=True) + EPSILON)
    return (rows * scale * gain, scale)


def norm_back(grad, rows, scale, gain):
    unit = rows * scale
    grad_gain = jnp.sum(grad * unit, axis=0)
    inner = grad * gain
    return (scale * (inner - unit * jnp.mean(inner * unit, axis=-1, keepdims=True)), grad_gain)


def layout(docs):
    place = jnp.arange(ROWS, dtype=jnp.int32)
    apart = place[:, None] - place[None, :]
    allowed = (apart >= 0)[None] & (docs[:, :, None] == docs[:, None, :])
    bucket = jnp.clip(apart, 0, BUCKETS - 1)
    table = (bucket[:, :, None] == jnp.arange(BUCKETS, dtype=jnp.int32)[None, None, :]).astype(
        jnp.bfloat16
    )
    return (allowed, table)


def score_of(queries, keys, bias, allowed, table):
    scores = einsum("mqhd,mkhd->mhqk", queries, keys) * FACTOR
    scores = scores + einsum("hb,qkb->hqk", bias, table)[None]
    return jnp.where(allowed[:, None], scores, -1000000000.0)


def attention_forward(rows, gain, bias, wqkv, wout, allowed, table):
    count = rows.shape[0]
    normed_full, scale = normalize(rows, gain)
    normed = normed_full.astype(jnp.bfloat16)
    mixed = product(normed, wqkv).astype(jnp.bfloat16).reshape(-1, ROWS, 3, HEADS, HEAD_DIM)
    queries, keys, values = (mixed[:, :, 0], mixed[:, :, 1], mixed[:, :, 2])
    scores = score_of(queries, keys, bias, allowed, table)
    top = jnp.max(scores, axis=-1, keepdims=True)
    raised = jnp.exp(scores - top)
    attend = raised / jnp.sum(raised, axis=-1, keepdims=True)
    context = einsum("mhqk,mkhd->mqhd", attend.astype(jnp.bfloat16), values)
    context = context.reshape(count, D).astype(jnp.bfloat16)
    return (product(context, wout), (scale, normed, queries, keys, values, context, attend))


def attention_back(grad, rows, gain, wqkv, wout, table, kept):
    scale, normed, queries, keys, values, context, attend = kept
    count = rows.shape[0]
    grad_low = grad.astype(jnp.bfloat16)
    grad_context = (
        product_right(grad_low, wout).astype(jnp.bfloat16).reshape(-1, ROWS, HEADS, HEAD_DIM)
    )
    grad_values = einsum("mhqk,mqhd->mkhd", attend.astype(jnp.bfloat16), grad_context)
    grad_attend = einsum("mqhd,mkhd->mhqk", grad_context, values)
    grad_scores = attend * (grad_attend - jnp.sum(attend * grad_attend, axis=-1, keepdims=True))
    scores_low = grad_scores.astype(jnp.bfloat16)
    grad_bias = jnp.sum(einsum("mhqk,qkb->mhb", scores_low, table), axis=0)
    grad_queries = einsum("mhqk,mkhd->mqhd", scores_low, keys) * FACTOR
    grad_keys = einsum("mhqk,mqhd->mkhd", scores_low, queries) * FACTOR
    grad_mixed = jnp.concatenate(
        [
            item.reshape(count, D).astype(jnp.bfloat16)
            for item in (grad_queries, grad_keys, grad_values)
        ],
        axis=1,
    )
    grad_normed = product_right(grad_mixed, wqkv)
    grad_rows, grad_gain = norm_back(grad_normed, rows, scale, gain)
    return (
        grad_rows,
        (grad_gain, grad_bias.reshape(-1), (normed, grad_mixed), (context, grad_low)),
    )


def feed_forward(rows, gain, w_gate, w_up, w_down):
    normed_full, scale = normalize(rows, gain)
    normed = normed_full.astype(jnp.bfloat16)
    gate = product(normed, w_gate)
    up_part = product(normed, w_up)
    hidden = (jax.nn.gelu(gate, approximate=False) * up_part).astype(jnp.bfloat16)
    return (product(hidden, w_down), (scale, normed, gate, up_part, hidden))


def feed_back(grad, rows, gain, w_gate, w_up, w_down, kept):
    scale, normed, gate, up_part, hidden = kept
    grad_low = grad.astype(jnp.bfloat16)
    grad_hidden = product_right(grad_low, w_down)
    grad_gate = (grad_hidden * up_part * gelu_slope(gate)).astype(jnp.bfloat16)
    grad_up = (grad_hidden * jax.nn.gelu(gate, approximate=False)).astype(jnp.bfloat16)
    grad_normed = product_right(grad_gate, w_gate) + product_right(grad_up, w_up)
    grad_rows, grad_gain = norm_back(grad_normed, rows, scale, gain)
    return (grad_rows, (grad_gain, (normed, grad_gate), (normed, grad_up), (hidden, grad_low)))


def route_table(ids, experts, capacity):
    flat = ids.reshape(MICRO, -1)
    hits = (flat[:, :, None] == jnp.arange(experts, dtype=jnp.int32)).astype(jnp.float32)
    count = flat.shape[1]
    earlier = jnp.tril(jnp.ones((count, count), jnp.bfloat16), -1)
    before = einsum("rs,mse->mre", earlier, hits.astype(jnp.bfloat16))
    slot = jnp.sum(before * hits, axis=2).astype(jnp.int32)
    batch = jnp.arange(MICRO, dtype=jnp.int32)[:, None]
    target = ((flat * MICRO + batch) * capacity + slot).reshape(-1)
    return (
        target[:, None] == jnp.arange(capacity * experts * MICRO, dtype=jnp.int32)[None, :]
    ).astype(jnp.bfloat16)


def body(
    tokens,
    cotangent,
    doc_ids,
    expert_ids,
    gate_logits,
    gain_attn_a,
    gain_mlp,
    gain_attn_b,
    gain_moe,
    bias_a,
    bias_b,
    qkv_a,
    out_a,
    w_gate,
    w_up,
    w_down,
    qkv_b,
    out_b,
    expert_in,
    expert_out,
):
    columns = lax.axis_size("expert")
    layers = lax.axis_size("dp")
    experts = columns * EXP_DEV
    capacity = (2 * ROWS + experts - 1) // experts + 1
    owners = layers * columns
    cube = Cube(layers, columns)
    small = (gain_attn_a, gain_mlp, gain_attn_b, gain_moe, bias_a, bias_b)
    sizes = [item.shape[0] for item in small]
    matrices = (qkv_a, w_gate, w_up, w_down, out_a, qkv_b, out_b)
    whole_tiles = qkv_a.shape[0] % 8 == 0

    packed = jnp.concatenate(small)
    packed = jnp.pad(packed, (0, 128 - packed.shape[0]))
    if whole_tiles:
        tile = jnp.broadcast_to(packed[None], (16, 128))
        full = gather_all(cube, matrices + (tile,))
        smalls = full[7].reshape(owners, 16, 128)[:, 0]
    else:
        full = [lax.all_gather(item, AXES, axis=0, tiled=True) for item in matrices]
        smalls = lax.all_gather(packed, AXES, axis=0)
    qkv_a, w_gate, w_up, w_down, out_a, qkv_b, out_b = full[:7]
    parts, start = [], 0
    for size in sizes:
        parts.append(smalls[:, start : start + size].reshape(-1))
        start += size
    gains = [item.astype(jnp.float32) for item in parts[:4]]
    bias_one, bias_two = (item.reshape(HEADS, BUCKETS) for item in parts[4:])

    rows = tokens.astype(jnp.float32)
    grad = cotangent.astype(jnp.float32)
    mix = jax.nn.softmax(gate_logits, axis=-1)
    allowed, table = layout(doc_ids)
    route = route_table(expert_ids, experts, capacity)
    per_device = EXP_DEV * MICRO * capacity

    def dispatch(values):
        sent = product_left(route, values).astype(jnp.bfloat16)
        sent = sent.reshape(columns, per_device, D)
        arrived = lax.all_to_all(sent, "expert", split_axis=0, concat_axis=0, tiled=True)
        whole = lax.all_gather(arrived, "dp", axis=0, tiled=True)
        whole = whole.reshape(owners, EXP_DEV, MICRO * capacity, D)
        return whole.transpose(1, 0, 2, 3).reshape(EXP_DEV, -1, D)

    def collect(term):
        term = term.astype(jnp.bfloat16).reshape(EXP_DEV, owners, MICRO * capacity, D)
        term = term.transpose(1, 0, 2, 3).reshape(owners, per_device, D)
        summed = lax.psum_scatter(term, "dp", scatter_dimension=0, tiled=True)
        back = lax.all_to_all(summed, "expert", split_axis=0, concat_axis=0, tiled=True)
        return product(route, back.reshape(columns * per_device, D)).reshape(-1, 2, D)

    grad_route = (grad[:, None, :] * mix[:, :, None]).reshape(-1, D).astype(jnp.bfloat16)
    grad_all = dispatch(grad_route)

    attn_one, kept_one = attention_forward(
        rows, gains[0], bias_one, qkv_a, out_a, allowed, table
    )
    first = rows + attn_one
    ffn, kept_ffn = feed_forward(first, gains[1], w_gate, w_up, w_down)
    middle = first + ffn
    attn_two, kept_two = attention_forward(
        middle, gains[2], bias_two, qkv_b, out_b, allowed, table
    )
    second = middle + attn_two
    normed_full, scale_moe = normalize(second, gains[3])
    normed = normed_full.astype(jnp.bfloat16)
    slot_all = dispatch(jnp.repeat(normed, 2, axis=0))
    pre = einsum("erd,edf->erf", slot_all, expert_in)
    act = jax.nn.gelu(pre, approximate=False).astype(jnp.bfloat16)
    per_route = collect(einsum("erf,efd->erd", act, expert_out))
    moe = jnp.sum(per_route * mix[:, :, None], axis=1)
    result = (second + moe).astype(jnp.bfloat16)

    grad_second = einsum("erf,erd->efd", act, grad_all)
    grad_act = einsum("erd,efd->erf", grad_all, expert_out)
    grad_pre = (grad_act * gelu_slope(pre)).astype(jnp.bfloat16)
    grad_first = einsum("erd,erf->edf", slot_all, grad_pre)
    grad_normed = jnp.sum(collect(einsum("erf,edf->erd", grad_pre, expert_in)), axis=1)
    grad_norm_rows, grad_gain_moe = norm_back(grad_normed, second, scale_moe, gains[3])
    grad_second_rows = grad + grad_norm_rows
    back_two, grads_two = attention_back(
        grad_second_rows, middle, gains[2], qkv_b, out_b, table, kept_two
    )
    grad_middle = grad_second_rows + back_two
    back_ffn, grads_ffn = feed_back(
        grad_middle, first, gains[1], w_gate, w_up, w_down, kept_ffn
    )
    grad_first_rows = grad_middle + back_ffn
    back_one, grads_one = attention_back(
        grad_first_rows, rows, gains[0], qkv_a, out_a, table, kept_one
    )
    grad_tokens = grad_first_rows + back_one

    small_grads = (
        grads_one[0],
        grads_ffn[0],
        grads_two[0],
        grad_gain_moe,
        grads_one[1],
        grads_two[1],
    )
    pairs = (
        grads_one[2],
        grads_ffn[1],
        grads_ffn[2],
        grads_ffn[3],
        grads_one[3],
        grads_two[2],
        grads_two[3],
    )
    terms = [product_left(left, right).astype(jnp.bfloat16) for left, right in pairs]
    terms = [item.reshape(owners, -1, item.shape[-1]) for item in terms]
    shared = jnp.concatenate([item.reshape(owners, -1) for item in small_grads], axis=1)
    shared = jnp.pad(shared, ((0, 0), (0, 128 - shared.shape[1])))
    if whole_tiles:
        tile = jnp.broadcast_to(shared[:, None], (owners, 8, 128))
        sums = reduce_all(cube, terms + [tile])
        own_small = sums[7][0]
    else:
        sums = [
            lax.psum_scatter(item, AXES, scatter_dimension=0, tiled=False).astype(jnp.float32)
            for item in terms
        ]
        own_small = lax.psum_scatter(shared, AXES, scatter_dimension=0, tiled=False)
    outs, start = [], 0
    for size in sizes:
        outs.append(own_small[start : start + size])
        start += size
    g_qkv_a, g_gate, g_up, g_down, g_out_a, g_qkv_b, g_out_b = sums[:7]
    return (
        (result, grad_tokens)
        + tuple(outs)
        + (g_qkv_a, g_out_a, g_gate, g_up, g_down, g_qkv_b, g_out_b)
        + (grad_first, grad_second)
    )


def solution(mesh):
    placed = (
        P(("dp", "expert"), None),
        P(("dp", "expert"), None),
        P(("dp", "expert"), None),
        P(("dp", "expert"), None),
        P(("dp", "expert"), None),
        P(("dp", "expert")),
        P(("dp", "expert")),
        P(("dp", "expert")),
        P(("dp", "expert")),
        P(("dp", "expert")),
        P(("dp", "expert")),
        P(("dp", "expert"), None),
        P(("dp", "expert"), None),
        P(("dp", "expert"), None),
        P(("dp", "expert"), None),
        P(("dp", "expert"), None),
        P(("dp", "expert"), None),
        P(("dp", "expert"), None),
        P("expert", None, "dp"),
        P("expert", "dp", None),
    )
    return jax.shard_map(
        body,
        mesh=mesh,
        in_specs=placed,
        out_specs=(
            P(("dp", "expert"), None),
            P(("dp", "expert"), None),
            P(("dp", "expert")),
            P(("dp", "expert")),
            P(("dp", "expert")),
            P(("dp", "expert")),
            P(("dp", "expert")),
            P(("dp", "expert")),
            P(("dp", "expert"), None),
            P(("dp", "expert"), None),
            P(("dp", "expert"), None),
            P(("dp", "expert"), None),
            P(("dp", "expert"), None),
            P(("dp", "expert"), None),
            P(("dp", "expert"), None),
            P("expert", None, "dp"),
            P("expert", "dp", None),
        ),
        check_vma=False,
    )
```

```python
import functools
import math

import jax
import jax.numpy as jnp
from jax import lax
from jax.experimental import pallas as pl
from jax.experimental.pallas import tpu as pltpu
from jax.sharding import PartitionSpec as P

D = 768
HEADS = 12
HEAD_DIM = 64
BUCKETS = 32
EXP_DEV = 4
ROWS = 64
MICRO = 2
AXES = ("dp", "expert")
MESH = pl.DeviceIdType.MESH

EPSILON = 1e-06
ROOT_HALF = 0.7071067811865476
ROOT_TWO_PI = 0.3989422804014327
FACTOR = 1.0 / math.sqrt(HEAD_DIM)


class Cube:
    def __init__(self, dp, expert):
        self.low = expert.bit_length() - 1
        self.bits = (dp * expert).bit_length() - 1
        self.sizes = (dp, expert)
        self.core = self.bits - self.low - 1

    def coordinates(self):
        dp, expert = lax.axis_index("dp"), lax.axis_index("expert")
        out = []
        for bit in range(self.bits):
            shift = self.bits - 1 - bit
            if shift >= self.low:
                out.append(lax.rem(lax.div(dp, 1 << (shift - self.low)), 2))
            else:
                out.append(lax.rem(lax.div(expert, 1 << shift), 2))
        return out

    def partner(self, bit, here):
        dp, expert = lax.axis_index("dp"), lax.axis_index("expert")
        shift = self.bits - 1 - bit
        if shift >= self.low:
            step = 1 << (shift - self.low)
            return (dp + step - 2 * step * here[bit], expert)
        step = 1 << shift
        return (dp, expert + step - 2 * step * here[bit])

    def orders(self):
        others = [bit for bit in range(self.core)]
        inner = [bit for bit in range(self.core + 1, self.bits)]
        first = inner[:-1] + inner[-1:] + others + [self.core]
        second = inner[:-1] + others + inner[-1:] + [self.core]
        return (first, second)

    def greet(self, here):
        barrier = pltpu.get_barrier_semaphore()
        for bit in range(self.bits):
            pl.semaphore_signal(
                barrier, inc=1, device_id=self.partner(bit, here), device_id_type=MESH
            )
        pl.semaphore_wait(barrier, self.bits)


def gather_kernel(cube, count, *refs):
    sources, outs = refs[:count], refs[count : 2 * count]
    local_sem, send_sem, recv_sem = refs[2 * count :]
    here = cube.coordinates()
    orders = cube.orders()
    own = []
    for index in range(count):
        copy = pltpu.make_async_copy(
            sources[index], outs[index].at[tuple(here)], local_sem.at[index]
        )
        copy.start()
        own.append(copy)
    cube.greet(here)
    going = [None] * count
    for tick in range(cube.bits + (count - 1) // 2 + 1):
        for index in range(count):
            stage = tick - index // 2
            if not 0 <= stage <= cube.bits:
                continue
            if stage == 0:
                own[index].wait()
            else:
                going[index].wait()
            if stage == cube.bits:
                continue
            order = orders[index % 2]
            done = order[:stage]
            place = tuple(slice(None) if b in done else here[b] for b in range(cube.bits))
            block = outs[index].at[place]
            copy = pltpu.make_async_remote_copy(
                src_ref=block,
                dst_ref=block,
                send_sem=send_sem.at[index, stage],
                recv_sem=recv_sem.at[index, stage],
                device_id=cube.partner(order[stage], here),
                device_id_type=MESH,
            )
            copy.start()
            going[index] = copy


def gather_all(cube, shards):
    count = len(shards)
    lead = (2,) * cube.bits
    full = pl.pallas_call(
        functools.partial(gather_kernel, cube, count),
        out_shape=[jax.ShapeDtypeStruct(lead + s.shape, s.dtype) for s in shards],
        in_specs=[pl.BlockSpec(memory_space=pl.ANY)] * count,
        out_specs=[pl.BlockSpec(memory_space=pl.ANY)] * count,
        scratch_shapes=[
            pltpu.SemaphoreType.DMA((count,)),
            pltpu.SemaphoreType.DMA((count, cube.bits)),
            pltpu.SemaphoreType.DMA((count, cube.bits)),
        ],
        compiler_params=pltpu.CompilerParams(collective_id=0, has_side_effects=True),
    )(*shards)
    return [f.reshape((-1,) + f.shape[-1:]) for f in full]


def reduce_kernel(cube, count, *refs):
    sources, outs = refs[:count], refs[count : 2 * count]
    rest = refs[2 * count :]
    totals = rest[:count]
    slots = [
        rest[count + index * cube.bits : count + (index + 1) * cube.bits] for index in range(count)
    ]
    local_sem, send_sem, recv_sem = rest[count + count * cube.bits :]
    here = cube.coordinates()
    orders = [list(reversed(order)) for order in cube.orders()]
    core = cube.core
    own = []
    for index in range(count):
        place = tuple(here[b] if b == core else slice(None) for b in range(cube.bits))
        copy = pltpu.make_async_copy(
            sources[index].at[place], totals[index], local_sem.at[index]
        )
        copy.start()
        own.append(copy)
    cube.greet(here)
    going = [None] * count
    others = [b for b in range(cube.bits) if b != core]

    def add(index, stage):
        order = orders[index % 2]
        done = order[: stage + 1]
        live = [b for b in others if b not in done]
        slot, total = slots[index][stage], totals[index]
        if not live:
            outs[index][...] = total[tuple(here[b] for b in others)].astype(jnp.float32) + slot[
                ...
            ].astype(jnp.float32)
            return

        def step(k, carry):
            where, inner = {}, []
            for position, b in enumerate(live):
                where[b] = lax.rem(lax.div(k, 1 << (len(live) - 1 - position)), 2)
                inner.append(where[b])
            at = tuple(where[b] if b in where else here[b] for b in others)
            left = total[at].astype(jnp.float32)
            right = slot[tuple(inner)].astype(jnp.float32)
            total[at] = (left + right).astype(total.dtype)
            return carry

        lax.fori_loop(0, 1 << len(live), step, 0)

    for tick in range(cube.bits + (count - 1) // 2 + 1):
        for index in range(count):
            stage = tick - index // 2
            if not 0 <= stage <= cube.bits:
                continue
            order = orders[index % 2]
            if stage > 0:
                if stage == 1:
                    own[index].wait()
                going[index].wait()
                add(index, stage - 1)
            if stage == cube.bits:
                continue
            bit = order[stage]
            done = order[:stage]
            if stage == 0:
                place = tuple(1 - here[b] if b == bit else slice(None) for b in range(cube.bits))
                block = sources[index].at[place]
            else:
                place = tuple(
                    1 - here[b] if b == bit else (here[b] if b in done else slice(None))
                    for b in others
                )
                block = totals[index].at[place]
            copy = pltpu.make_async_remote_copy(
                src_ref=block,
                dst_ref=slots[index][stage],
                send_sem=send_sem.at[index, stage],
                recv_sem=recv_sem.at[index, stage],
                device_id=cube.partner(bit, here),
                device_id_type=MESH,
            )
            copy.start()
            going[index] = copy


def reduce_all(cube, wholes):
    count = len(wholes)
    lead = (2,) * cube.bits
    shapes = [w.shape[1:] for w in wholes]
    wholes = [w.reshape(lead + w.shape[1:]) for w in wholes]
    scratch = [
        pltpu.VMEM((2,) * (cube.bits - 1) + shape, w.dtype) for shape, w in zip(shapes, wholes)
    ]
    for shape, w in zip(shapes, wholes):
        for stage in range(cube.bits):
            scratch.append(pltpu.VMEM((2,) * (cube.bits - 1 - stage) + shape, w.dtype))
    return pl.pallas_call(
        functools.partial(reduce_kernel, cube, count),
        out_shape=[jax.ShapeDtypeStruct(shape, jnp.float32) for shape in shapes],
        in_specs=[pl.BlockSpec(memory_space=pl.ANY)] * count,
        out_specs=[pl.BlockSpec(memory_space=pltpu.VMEM)] * count,
        scratch_shapes=scratch
        + [
            pltpu.SemaphoreType.DMA((count,)),
            pltpu.SemaphoreType.DMA((count, cube.bits)),
            pltpu.SemaphoreType.DMA((count, cube.bits)),
        ],
        compiler_params=pltpu.CompilerParams(
            collective_id=1, has_side_effects=True, vmem_limit_bytes=58 * 2**20
        ),
    )(*wholes)


def product(left, right):
    return jnp.dot(left, right, preferred_element_type=jnp.float32)


def product_left(left, right):
    return lax.dot_general(
        left, right, (((0,), (0,)), ((), ())), preferred_element_type=jnp.float32
    )


def product_right(left, right):
    return lax.dot_general(
        left, right, (((1,), (1,)), ((), ())), preferred_element_type=jnp.float32
    )


def einsum(spec, left, right):
    return jnp.einsum(spec, left, right, preferred_element_type=jnp.float32)


def gelu_slope(values):
    return (
        0.5 * (1.0 + lax.erf(values * ROOT_HALF))
        + values * jnp.exp(-0.5 * values * values) * ROOT_TWO_PI
    )


def normalize(rows, gain):
    scale = lax.rsqrt(jnp.mean(rows * rows, axis=-1, keepdims=True) + EPSILON)
    return (rows * scale * gain, scale)


def norm_back(grad, rows, scale, gain):
    unit = rows * scale
    grad_gain = jnp.sum(grad * unit, axis=0)
    inner = grad * gain
    return (scale * (inner - unit * jnp.mean(inner * unit, axis=-1, keepdims=True)), grad_gain)


def layout(docs):
    place = jnp.arange(ROWS, dtype=jnp.int32)
    apart = place[:, None] - place[None, :]
    allowed = (apart >= 0)[None] & (docs[:, :, None] == docs[:, None, :])
    bucket = jnp.clip(apart, 0, BUCKETS - 1)
    table = (bucket[:, :, None] == jnp.arange(BUCKETS, dtype=jnp.int32)[None, None, :]).astype(
        jnp.bfloat16
    )
    return (allowed, table)


def score_of(queries, keys, bias, allowed, table):
    scores = einsum("mqhd,mkhd->mhqk", queries, keys) * FACTOR
    scores = scores + einsum("hb,qkb->hqk", bias, table)[None]
    return jnp.where(allowed[:, None], scores, -1000000000.0)


def attention_forward(rows, gain, bias, wqkv, wout, allowed, table):
    count = rows.shape[0]
    normed_full, scale = normalize(rows, gain)
    normed = normed_full.astype(jnp.bfloat16)
    mixed = product(normed, wqkv).astype(jnp.bfloat16).reshape(-1, ROWS, 3, HEADS, HEAD_DIM)
    queries, keys, values = (mixed[:, :, 0], mixed[:, :, 1], mixed[:, :, 2])
    scores = score_of(queries, keys, bias, allowed, table)
    top = jnp.max(scores, axis=-1, keepdims=True)
    raised = jnp.exp(scores - top)
    attend = raised / jnp.sum(raised, axis=-1, keepdims=True)
    context = einsum("mhqk,mkhd->mqhd", attend.astype(jnp.bfloat16), values)
    context = context.reshape(count, D).astype(jnp.bfloat16)
    return (product(context, wout), (scale, normed, queries, keys, values, context, attend))


def attention_back(grad, rows, gain, wqkv, wout, table, kept):
    scale, normed, queries, keys, values, context, attend = kept
    count = rows.shape[0]
    grad_low = grad.astype(jnp.bfloat16)
    grad_context = (
        product_right(grad_low, wout).astype(jnp.bfloat16).reshape(-1, ROWS, HEADS, HEAD_DIM)
    )
    grad_values = einsum("mhqk,mqhd->mkhd", attend.astype(jnp.bfloat16), grad_context)
    grad_attend = einsum("mqhd,mkhd->mhqk", grad_context, values)
    grad_scores = attend * (grad_attend - jnp.sum(attend * grad_attend, axis=-1, keepdims=True))
    scores_low = grad_scores.astype(jnp.bfloat16)
    grad_bias = jnp.sum(einsum("mhqk,qkb->mhb", scores_low, table), axis=0)
    grad_queries = einsum("mhqk,mkhd->mqhd", scores_low, keys) * FACTOR
    grad_keys = einsum("mhqk,mqhd->mkhd", scores_low, queries) * FACTOR
    grad_mixed = jnp.concatenate(
        [
            item.reshape(count, D).astype(jnp.bfloat16)
            for item in (grad_queries, grad_keys, grad_values)
        ],
        axis=1,
    )
    grad_normed = product_right(grad_mixed, wqkv)
    grad_rows, grad_gain = norm_back(grad_normed, rows, scale, gain)
    return (
        grad_rows,
        (grad_gain, grad_bias.reshape(-1), (normed, grad_mixed), (context, grad_low)),
    )


def feed_forward(rows, gain, w_gate, w_up, w_down):
    normed_full, scale = normalize(rows, gain)
    normed = normed_full.astype(jnp.bfloat16)
    gate = product(normed, w_gate)
    up_part = product(normed, w_up)
    hidden = (jax.nn.gelu(gate, approximate=False) * up_part).astype(jnp.bfloat16)
    return (product(hidden, w_down), (scale, normed, gate, up_part, hidden))


def feed_back(grad, rows, gain, w_gate, w_up, w_down, kept):
    scale, normed, gate, up_part, hidden = kept
    grad_low = grad.astype(jnp.bfloat16)
    grad_hidden = product_right(grad_low, w_down)
    grad_gate = (grad_hidden * up_part * gelu_slope(gate)).astype(jnp.bfloat16)
    grad_up = (grad_hidden * jax.nn.gelu(gate, approximate=False)).astype(jnp.bfloat16)
    grad_normed = product_right(grad_gate, w_gate) + product_right(grad_up, w_up)
    grad_rows, grad_gain = norm_back(grad_normed, rows, scale, gain)
    return (grad_rows, (grad_gain, (normed, grad_gate), (normed, grad_up), (hidden, grad_low)))


def route_table(ids, experts, capacity):
    flat = ids.reshape(MICRO, -1)
    hits = (flat[:, :, None] == jnp.arange(experts, dtype=jnp.int32)).astype(jnp.float32)
    count = flat.shape[1]
    earlier = jnp.tril(jnp.ones((count, count), jnp.bfloat16), -1)
    before = einsum("rs,mse->mre", earlier, hits.astype(jnp.bfloat16))
    slot = jnp.sum(before * hits, axis=2).astype(jnp.int32)
    batch = jnp.arange(MICRO, dtype=jnp.int32)[:, None]
    target = ((flat * MICRO + batch) * capacity + slot).reshape(-1)
    return (
        target[:, None] == jnp.arange(capacity * experts * MICRO, dtype=jnp.int32)[None, :]
    ).astype(jnp.bfloat16)


def body(
    tokens,
    cotangent,
    doc_ids,
    expert_ids,
    gate_logits,
    gain_attn_a,
    gain_mlp,
    gain_attn_b,
    gain_moe,
    bias_a,
    bias_b,
    qkv_a,
    out_a,
    w_gate,
    w_up,
    w_down,
    qkv_b,
    out_b,
    expert_in,
    expert_out,
):
    columns = lax.axis_size("expert")
    layers = lax.axis_size("dp")
    experts = columns * EXP_DEV
    capacity = (2 * ROWS + experts - 1) // experts + 1
    owners = layers * columns
    cube = Cube(layers, columns)
    small = (gain_attn_a, gain_mlp, gain_attn_b, gain_moe, bias_a, bias_b)
    sizes = [item.shape[0] for item in small]
    matrices = (qkv_a, w_gate, w_up, w_down, out_a)
    whole_tiles = qkv_a.shape[0] % 8 == 0

    packed = jnp.concatenate(small)
    packed = jnp.pad(packed, (0, 128 - packed.shape[0]))
    if whole_tiles:
        tile = jnp.broadcast_to(packed[None], (16, 128))
        full = gather_all(cube, matrices + (tile,))
        smalls = full[5].reshape(owners, 16, 128)[:, 0]
    else:
        full = [lax.all_gather(item, AXES, axis=0, tiled=True) for item in matrices]
        smalls = lax.all_gather(packed, AXES, axis=0)
    qkv_a, w_gate, w_up, w_down, out_a = full[:5]
    qkv_b = lax.all_gather(qkv_b, AXES, axis=0, tiled=True)
    out_b = lax.all_gather(out_b, AXES, axis=0, tiled=True)
    parts, start = [], 0
    for size in sizes:
        parts.append(smalls[:, start : start + size].reshape(-1))
        start += size
    gains = [item.astype(jnp.float32) for item in parts[:4]]
    bias_one, bias_two = (item.reshape(HEADS, BUCKETS) for item in parts[4:])

    rows = tokens.astype(jnp.float32)
    grad = cotangent.astype(jnp.float32)
    mix = jax.nn.softmax(gate_logits, axis=-1)
    allowed, table = layout(doc_ids)
    route = route_table(expert_ids, experts, capacity)
    per_device = EXP_DEV * MICRO * capacity

    def dispatch(values):
        sent = product_left(route, values).astype(jnp.bfloat16)
        sent = sent.reshape(columns, per_device, D)
        arrived = lax.all_to_all(sent, "expert", split_axis=0, concat_axis=0, tiled=True)
        whole = lax.all_gather(arrived, "dp", axis=0, tiled=True)
        whole = whole.reshape(owners, EXP_DEV, MICRO * capacity, D)
        return whole.transpose(1, 0, 2, 3).reshape(EXP_DEV, -1, D)

    def collect_sum(term):
        term = term.astype(jnp.bfloat16).reshape(EXP_DEV, owners, MICRO * capacity, D)
        term = term.transpose(1, 0, 2, 3).reshape(owners, per_device, D)
        return lax.psum_scatter(term, "dp", scatter_dimension=0, tiled=True)

    def collect_back(summed):
        back = lax.all_to_all(summed, "expert", split_axis=0, concat_axis=0, tiled=True)
        return product(route, back.reshape(columns * per_device, D)).reshape(-1, 2, D)

    grad_route = (grad[:, None, :] * mix[:, :, None]).reshape(-1, D).astype(jnp.bfloat16)
    grad_all = dispatch(grad_route)

    attn_one, kept_one = attention_forward(
        rows, gains[0], bias_one, qkv_a, out_a, allowed, table
    )
    first = rows + attn_one
    ffn, kept_ffn = feed_forward(first, gains[1], w_gate, w_up, w_down)
    middle = first + ffn
    attn_two, kept_two = attention_forward(
        middle, gains[2], bias_two, qkv_b, out_b, allowed, table
    )
    second = middle + attn_two
    normed_full, scale_moe = normalize(second, gains[3])
    normed = normed_full.astype(jnp.bfloat16)
    slot_all = dispatch(jnp.repeat(normed, 2, axis=0))
    pre = einsum("erd,edf->erf", slot_all, expert_in)
    act = jax.nn.gelu(pre, approximate=False).astype(jnp.bfloat16)
    term = einsum("erf,efd->erd", act, expert_out).astype(jnp.bfloat16)

    grad_second = einsum("erf,erd->efd", act, grad_all)
    grad_act = einsum("erd,efd->erf", grad_all, expert_out)
    grad_pre = (grad_act * gelu_slope(pre)).astype(jnp.bfloat16)
    grad_first = einsum("erd,erf->edf", slot_all, grad_pre)
    summed_grad = collect_sum(einsum("erf,edf->erd", grad_pre, expert_in))
    term, summed_grad = lax.optimization_barrier((term, summed_grad))
    summed = collect_sum(term)
    grad_normed = jnp.sum(collect_back(summed_grad), axis=1)
    grad_norm_rows, grad_gain_moe = norm_back(grad_normed, second, scale_moe, gains[3])
    grad_second_rows = grad + grad_norm_rows
    back_two, grads_two = attention_back(
        grad_second_rows, middle, gains[2], qkv_b, out_b, table, kept_two
    )
    grad_middle = grad_second_rows + back_two
    grad_middle, summed = lax.optimization_barrier((grad_middle, summed))
    moe = jnp.sum(collect_back(summed) * mix[:, :, None], axis=1)
    result = (second + moe).astype(jnp.bfloat16)
    g_qkv_b, g_out_b = (
        lax.psum_scatter(
            product_left(left, right).astype(jnp.bfloat16), AXES, scatter_dimension=0, tiled=True
        ).astype(jnp.float32)
        for left, right in grads_two[2:4]
    )
    back_ffn, grads_ffn = feed_back(
        grad_middle, first, gains[1], w_gate, w_up, w_down, kept_ffn
    )
    grad_first_rows = grad_middle + back_ffn
    back_one, grads_one = attention_back(
        grad_first_rows, rows, gains[0], qkv_a, out_a, table, kept_one
    )
    grad_tokens = grad_first_rows + back_one

    small_grads = (
        grads_one[0],
        grads_ffn[0],
        grads_two[0],
        grad_gain_moe,
        grads_one[1],
        grads_two[1],
    )
    pairs = (
        grads_one[2],
        grads_ffn[1],
        grads_ffn[2],
        grads_ffn[3],
        grads_one[3],
    )
    terms = [product_left(left, right).astype(jnp.bfloat16) for left, right in pairs]
    terms = [item.reshape(owners, -1, item.shape[-1]) for item in terms]
    shared = jnp.concatenate([item.reshape(owners, -1) for item in small_grads], axis=1)
    shared = jnp.pad(shared, ((0, 0), (0, 128 - shared.shape[1])))
    if whole_tiles:
        tile = jnp.broadcast_to(shared[:, None], (owners, 8, 128))
        sums = reduce_all(cube, terms + [tile])
        own_small = sums[5][0]
    else:
        sums = [
            lax.psum_scatter(item, AXES, scatter_dimension=0, tiled=False).astype(jnp.float32)
            for item in terms
        ]
        own_small = lax.psum_scatter(shared, AXES, scatter_dimension=0, tiled=False)
    outs, start = [], 0
    for size in sizes:
        outs.append(own_small[start : start + size])
        start += size
    g_qkv_a, g_gate, g_up, g_down, g_out_a = sums[:5]
    return (
        (result, grad_tokens)
        + tuple(outs)
        + (g_qkv_a, g_out_a, g_gate, g_up, g_down, g_qkv_b, g_out_b)
        + (grad_first, grad_second)
    )


def solution(mesh):
    placed = (
        P(("dp", "expert"), None),
        P(("dp", "expert"), None),
        P(("dp", "expert"), None),
        P(("dp", "expert"), None),
        P(("dp", "expert"), None),
        P(("dp", "expert")),
        P(("dp", "expert")),
        P(("dp", "expert")),
        P(("dp", "expert")),
        P(("dp", "expert")),
        P(("dp", "expert")),
        P(("dp", "expert"), None),
        P(("dp", "expert"), None),
        P(("dp", "expert"), None),
        P(("dp", "expert"), None),
        P(("dp", "expert"), None),
        P(("dp", "expert"), None),
        P(("dp", "expert"), None),
        P("expert", None, "dp"),
        P("expert", "dp", None),
    )
    return jax.shard_map(
        body,
        mesh=mesh,
        in_specs=placed,
        out_specs=(
            P(("dp", "expert"), None),
            P(("dp", "expert"), None),
            P(("dp", "expert")),
            P(("dp", "expert")),
            P(("dp", "expert")),
            P(("dp", "expert")),
            P(("dp", "expert")),
            P(("dp", "expert")),
            P(("dp", "expert"), None),
            P(("dp", "expert"), None),
            P(("dp", "expert"), None),
            P(("dp", "expert"), None),
            P(("dp", "expert"), None),
            P(("dp", "expert"), None),
            P(("dp", "expert"), None),
            P("expert", None, "dp"),
            P("expert", "dp", None),
        ),
        check_vma=False,
    )
```
